512 devices in a mesh: ctx: 64 (over z, y_hi, core), head: 8 (over x, y_lo).
Axes of the slice: x: 4, y: 8 (y_hi: 4, y_lo: 2; y = y_hi * 2 + y_lo), z: 8, core: 2. Of those that a mesh axis runs over, the one named last changes fastest.
Arguments:
- query_rows: bfloat16 [32768, 4096], P('ctx', 'head'), may hold values from -43 to 43
- key_rows: bfloat16 [32768, 4096], P('ctx', 'head'), may hold values from -4 to 4
- value_rows: bfloat16 [32768, 4096], P('ctx', 'head'), may hold values from -16 to 16
- out_gain: float32 [4096], P('head'), may hold values from 0.5 to 1.5
Outputs:
- normed: bfloat16 [32768, 4096], P('ctx', 'head')
The draws below stay inside these ranges and needn't reach their ends.
All inputs are finite; a program needn't handle non-finite values.
Results may differ from the reference program's by a relative error of at most 0.0085.
Values may be sent and summed in bfloat16 or wider, within the bound.
No kernel may reach another device: no remote copies, remote signals or barrier semaphores. Data moves between devices by JAX's collectives and lax.ppermute only.
A program may use at most 64 MiB of HBM per device.

```python
import jax
import jax.numpy as jnp
from jax import lax

HEADS = 32
HEAD_DIM = 128
BLOCK = 256
SUMMARY = 16
TOKENS = 32768


def draw_key_rows(key, part):
    own_key = jax.random.fold_in(key, 1)
    drawn_rows = jnp.clip(jax.random.normal(own_key, (TOKENS, HEADS, HEAD_DIM), jnp.float32), -4.0, 4.0)
    return drawn_rows.reshape(TOKENS, HEADS * HEAD_DIM).astype(jnp.bfloat16)


def draw_query_rows(key, part):
    own_key = jax.random.fold_in(key, 2)
    drawn_rows = jnp.clip(jax.random.normal(own_key, (TOKENS, HEADS, HEAD_DIM), jnp.float32), -4.0, 4.0)
    return drawn_rows.reshape(TOKENS, HEADS * HEAD_DIM).astype(jnp.bfloat16)


def draw_value_rows(key, part):
    own_key = jax.random.fold_in(key, 3)
    head_place = jnp.arange(HEADS, dtype=jnp.float32) / (HEADS - 1)
    head_scale = 0.4 * jnp.power(10.0, head_place)
    drawn_rows = jnp.clip(jax.random.normal(own_key, (TOKENS, HEADS, HEAD_DIM), jnp.float32), -4.0, 4.0)
    drawn_rows = drawn_rows * head_scale[None, :, None]
    return drawn_rows.reshape(TOKENS, HEADS * HEAD_DIM).astype(jnp.bfloat16)


def setup_inputs(seed: int = 0) -> dict:
    key_list = jax.random.split(jax.random.key(seed), 5)
    query_rows = draw_query_rows(jax.random.fold_in(key_list[4], 71), 0)
    key_rows = draw_key_rows(jax.random.fold_in(key_list[4], 71), 0)
    value_rows = draw_value_rows(jax.random.fold_in(key_list[4], 71), 0)
    out_gain = jnp.clip(1.0 + 0.1 * jax.random.normal(key_list[3], (HEADS * HEAD_DIM,), jnp.float32), 0.5, 1.5)
    return {"query_rows": query_rows, "key_rows": key_rows, "value_rows": value_rows, "out_gain": out_gain}


def reference(query_rows, key_rows, value_rows, out_gain):
    total_rows = query_rows.shape[0]
    block_count = total_rows // BLOCK
    scale_factor = HEAD_DIM ** (-0.5)
    block_shape = (block_count, BLOCK, HEADS, HEAD_DIM)
    query_blocks = query_rows.reshape(block_shape)
    key_blocks = key_rows.reshape(block_shape)
    value_blocks = value_rows.reshape(block_shape)
    summary_keys = key_blocks[:, BLOCK - SUMMARY:].reshape(block_count * SUMMARY, HEADS, HEAD_DIM).astype(jnp.float32)
    summary_values = value_blocks[:, BLOCK - SUMMARY:].reshape(block_count * SUMMARY, HEADS, HEAD_DIM).astype(jnp.float32)
    summary_block = jnp.arange(block_count * SUMMARY, dtype=jnp.int32) // SUMMARY
    causal = jnp.arange(BLOCK, dtype=jnp.int32)[:, None] >= jnp.arange(BLOCK, dtype=jnp.int32)[None, :]

    def attend_block(block_items):
        query_part, key_part, value_part, block_index = block_items
        query_float = query_part.astype(jnp.float32)
        band_scores = jnp.einsum('qhd,khd->hqk', query_float, key_part.astype(jnp.float32)) * scale_factor
        remote = jnp.einsum('qhd,khd->hqk', query_float, summary_keys) * scale_factor
        band_mask = jnp.broadcast_to(causal[None], band_scores.shape)
        remote_mask = jnp.broadcast_to((summary_block < block_index)[None, None, :], remote.shape)
        scores = jnp.concatenate([band_scores, remote], axis=-1)
        allowed = jnp.concatenate([band_mask, remote_mask], axis=-1)
        scores = jnp.where(allowed, scores, -jnp.inf)
        row_max = lax.optimization_barrier(jnp.max(scores, axis=-1, keepdims=True))
        weights = jnp.where(allowed, jnp.exp(scores - row_max), 0.0)
        row_sum = lax.optimization_barrier(jnp.sum(weights, axis=-1))
        rounded = weights.astype(jnp.bfloat16)
        mixed_values = jnp.concatenate([value_part.astype(jnp.float32), summary_values], axis=0)
        summed = jnp.einsum('hqk,khd->qhd', rounded.astype(jnp.float32), mixed_values)
        return summed / jnp.transpose(row_sum)[:, :, None]
    attended = lax.map(attend_block, (query_blocks, key_blocks, value_blocks, jnp.arange(block_count, dtype=jnp.int32)))
    attended = attended.reshape(total_rows, HEADS * HEAD_DIM)
    mean_square = lax.optimization_barrier(jnp.mean(attended * attended, axis=-1, keepdims=True))
    return (attended * lax.rsqrt(mean_square + 1e-06) * out_gain).astype(jnp.bfloat16)
```

```python
import functools
import math

import jax
import jax.numpy as jnp
from jax import lax
from jax.experimental import pallas as pl
from jax.experimental.pallas import tpu as pltpu
from jax.sharding import PartitionSpec as P

HEAD_DIM = 128
BLOCK = 256
SUMMARY = 16
FEATURES = 4096
CHIPS_Z, CHIPS_Y, CORES = 8, 4, 2
SLAB = CHIPS_Y * CORES
HALF = 256
ROWS = 512
SCALE = HEAD_DIM**-0.5 * math.log2(math.e)
MINUS = -1e30
VIRTUAL = 4
VMEM = pl.BlockSpec(memory_space=pltpu.VMEM)
SMEM = pl.BlockSpec(memory_space=pltpu.SMEM)
LIMIT = 48 * 1024 * 1024

F32 = jnp.float32
BF16 = jnp.bfloat16


def rows_dot(a, b):
    return lax.dot_general(a, b, (((1,), (1,)), ((), ())), preferred_element_type=F32)


def columns_dot(a, b):
    return lax.dot_general(a, b, (((0,), (0,)), ((), ())), preferred_element_type=F32)


def pack_summary(key_ref, value_ref, out_ref):
    for core in range(CORES):
        columns = slice(core * HALF, (core + 1) * HALF)
        for start, ref in ((0, key_ref), (2 * SUMMARY, value_ref)):
            for block in range(2):
                end = (block + 1) * BLOCK
                piece = ref[end - SUMMARY : end, columns]
                first = start + block * SUMMARY
                for y in range(CHIPS_Y):
                    out_ref[y * CORES + core, first : first + SUMMARY] = piece


def pack_other(place_ref, query_ref, key_ref, value_ref, out_ref):
    other = pl.multiple_of((1 - place_ref[2]) * HALF, HALF)
    for part, ref in enumerate((query_ref, key_ref, value_ref)):
        out_ref[part * ROWS : (part + 1) * ROWS] = ref[:, pl.ds(other, HALF)]


def slab_keys(slab, head):
    columns = slice(head * HEAD_DIM, (head + 1) * HEAD_DIM)
    sources = slab.shape[0]
    keys = slab[:, : 2 * SUMMARY, columns].reshape(sources * 2 * SUMMARY, HEAD_DIM)
    values = slab[:, 2 * SUMMARY :, columns].reshape(sources * 2 * SUMMARY, HEAD_DIM)
    return keys, values


def fold_slab(queries, state, slab, first_blocks):
    max_ref, sum_ref, acc_ref = state
    for virtual in range(VIRTUAL):
        keys, values = slab_keys(slab, virtual % 2)
        scores = rows_dot(keys, queries[virtual]) * SCALE
        if first_blocks is not None:
            shape = scores.shape
            key_block = lax.broadcasted_iota(jnp.int32, shape, 0) // SUMMARY
            query_block = first_blocks[virtual // 2] + lax.broadcasted_iota(jnp.int32, shape, 1) // BLOCK
            allowed = key_block < query_block
            scores = jnp.where(allowed, scores, MINUS)
        old_max = max_ref[virtual]
        new_max = jnp.maximum(old_max, jnp.max(scores, axis=0, keepdims=True))
        weights = jnp.exp2(scores - new_max)
        shrink = jnp.exp2(old_max - new_max)
        max_ref[virtual] = new_max
        sum_ref[virtual] = sum_ref[virtual] * shrink + jnp.sum(weights, axis=0, keepdims=True)
        acc_ref[virtual] = acc_ref[virtual] * shrink + columns_dot(values, weights.astype(BF16))


def band(query_ref, key_ref, value_ref, mine, other_ref, state, queries_ref):
    max_ref, sum_ref, acc_ref = state
    shape = (BLOCK, BLOCK)
    causal = lax.broadcasted_iota(jnp.int32, shape, 0) <= lax.broadcasted_iota(jnp.int32, shape, 1)
    for virtual in range(VIRTUAL):
        owner, head = divmod(virtual, 2)
        for block in range(2):
            rows = slice(block * BLOCK, (block + 1) * BLOCK)
            if owner == 0:
                columns = pl.ds(mine + head * HEAD_DIM, HEAD_DIM)
                query, key, value = (ref[rows, columns] for ref in (query_ref, key_ref, value_ref))
            else:
                columns = slice(head * HEAD_DIM, (head + 1) * HEAD_DIM)
                query, key, value = (
                    other_ref[part * ROWS + block * BLOCK : part * ROWS + (block + 1) * BLOCK, columns]
                    for part in range(3)
                )
            queries_ref[virtual, rows] = query
            scores = jnp.where(causal, rows_dot(key, query) * SCALE, MINUS)
            new_max = jnp.max(scores, axis=0, keepdims=True)
            weights = jnp.exp2(scores - new_max)
            max_ref[virtual, :, rows] = new_max
            sum_ref[virtual, :, rows] = jnp.sum(weights, axis=0, keepdims=True)
            acc_ref[virtual, :, rows] = columns_dot(value, weights.astype(BF16))


def finish(core, state, own_ref, other_ref, square_ref):
    _, sum_ref, acc_ref = state
    for owner, ref in enumerate((own_ref, other_ref)):
        total = jnp.zeros((1, ROWS), F32)
        for head in range(2):
            virtual = owner * 2 + head
            attended = acc_ref[virtual] / sum_ref[virtual]
            ref[head] = attended
            total += jnp.sum(attended * attended, axis=0, keepdims=True)
        square_ref[core if owner == 0 else 1 - core] = jnp.broadcast_to(total, square_ref.shape[1:])


def attend_all(place_ref, query_ref, key_ref, value_ref, other_in_ref, slabs_ref, own_ref, other_ref, square_ref, *scratch):
    queries_ref, *state = scratch
    here, chip, core = place_ref[0], place_ref[1], place_ref[2]
    mine = pl.multiple_of(core * HALF, HALF)
    band(query_ref, key_ref, value_ref, mine, other_in_ref, state, queries_ref)
    first_blocks = [(chip * CORES + core) * 2, (chip * CORES + 1 - core) * 2]
    fold_slab(queries_ref, state, slabs_ref[here], first_blocks)

    @pl.loop(0, here)
    def _(z):
        fold_slab(queries_ref, state, slabs_ref[z], None)

    finish(core, state, own_ref, other_ref, square_ref)


def scale_rows(place_ref, own_ref, other_ref, square_ref, gain_ref, out_ref):
    core = place_ref[2]
    total = jnp.sum(square_ref[...], axis=0, keepdims=True)
    scale = lax.rsqrt(total * (1.0 / FEATURES) + 1e-06)
    for owner, ref in enumerate((own_ref, other_ref)):
        first = pl.multiple_of((core if owner == 0 else 1 - core) * HALF, HALF)
        for head in range(2):
            columns = pl.ds(first + head * HEAD_DIM, HEAD_DIM)
            rows = jnp.transpose(ref[head] * scale)
            out_ref[:, columns] = (rows * gain_ref[:, columns]).astype(BF16)


def call(body, out_shape, in_specs, scratch=(), cost=None, **more):
    outs = jax.tree.map(lambda _: VMEM, out_shape)
    return pl.pallas_call(
        body,
        out_shape=out_shape,
        in_specs=in_specs,
        out_specs=outs,
        scratch_shapes=list(scratch),
        cost_estimate=cost,
        compiler_params=pltpu.CompilerParams(vmem_limit_bytes=LIMIT),
        **more,
    )


def groups(axes):
    made = {}
    for index in range(CHIPS_Z * SLAB):
        coordinate = {"z": index // SLAB, "y": index // CORES % CHIPS_Y, "c": index % CORES}
        made.setdefault(tuple(v for k, v in coordinate.items() if k not in axes), []).append(index)
    return list(made.values())


def swap_cores(array):
    pairs = [(index, index ^ 1) for index in range(CHIPS_Z * SLAB)]
    return lax.ppermute(array, "ctx", pairs)


def local(head_count, query_rows, key_rows, value_rows, out_gain):
    index = lax.axis_index("ctx")
    place = jnp.stack([index >> 3, (index >> 1) & (CHIPS_Y - 1), index & 1]).astype(jnp.int32)

    packed = call(pack_summary, jax.ShapeDtypeStruct((SLAB, 4 * SUMMARY, HALF), BF16), [VMEM] * 2)(key_rows, value_rows)
    slab = lax.all_to_all(packed, "ctx", 0, 0, axis_index_groups=groups("yc"), tiled=True)
    to_other = call(pack_other, jax.ShapeDtypeStruct((3 * ROWS, HALF), BF16), [SMEM] + [VMEM] * 3)(
        place, query_rows, key_rows, value_rows
    )
    from_other = swap_cores(to_other)
    slabs = lax.all_to_all(
        jnp.broadcast_to(slab[None], (CHIPS_Z, *slab.shape)), "ctx", 0, 0, axis_index_groups=groups("z"), tiled=True
    )

    attended = jax.ShapeDtypeStruct((2, HEAD_DIM, ROWS), F32)
    own, other, squares = call(
        attend_all,
        (attended, attended, jax.ShapeDtypeStruct((CORES, head_count, ROWS), F32)),
        [SMEM] + [VMEM] * 5,
        scratch=[
            pltpu.VMEM((VIRTUAL, ROWS, HEAD_DIM), BF16),
            pltpu.VMEM((VIRTUAL, 1, ROWS), F32),
            pltpu.VMEM((VIRTUAL, 1, ROWS), F32),
            pltpu.VMEM((VIRTUAL, HEAD_DIM, ROWS), F32),
        ],
    )(place, query_rows, key_rows, value_rows, from_other, slabs)
    back = swap_cores(other)
    chips = [
        [(chip * CORES + core) * head_count + head for core in range(CORES) for head in range(head_count)]
        for chip in range(CHIPS_Z * CHIPS_Y)
    ]
    totals = lax.all_to_all(
        squares.reshape(CORES * head_count, ROWS), ("ctx", "head"), 0, 0, axis_index_groups=chips, tiled=True
    )
    return call(scale_rows, jax.ShapeDtypeStruct((ROWS, 4 * HEAD_DIM), BF16), [SMEM] + [VMEM] * 4)(
        place, own, back, totals, out_gain[None]
    )


def solution(mesh):
    placed = (P("ctx", "head"), P("ctx", "head"), P("ctx", "head"), P("head"))
    return jax.shard_map(
        functools.partial(local, mesh.shape["head"]),
        mesh=mesh,
        in_specs=placed,
        out_specs=P("ctx", "head"),
        check_vma=False,
    )
```

```python
import functools
import math

import jax
import jax.numpy as jnp
from jax import lax
from jax.experimental import pallas as pl
from jax.experimental.pallas import tpu as pltpu
from jax.sharding import PartitionSpec as P

HEAD_DIM = 128
BLOCK = 256
SUMMARY = 16
FEATURES = 4096
CHIPS_Z, CHIPS_Y, CORES = 8, 4, 2
SLAB = CHIPS_Y * CORES
HALF = 256
ROWS = 512
SCALE = HEAD_DIM**-0.5 * math.log2(math.e)
MINUS = -1e30
VIRTUAL = 4
VMEM = pl.BlockSpec(memory_space=pltpu.VMEM)
SMEM = pl.BlockSpec(memory_space=pltpu.SMEM)
LIMIT = 48 * 1024 * 1024

F32 = jnp.float32
BF16 = jnp.bfloat16


def rows_dot(a, b):
    return lax.dot_general(a, b, (((1,), (1,)), ((), ())), preferred_element_type=F32)


def columns_dot(a, b):
    return lax.dot_general(a, b, (((0,), (0,)), ((), ())), preferred_element_type=F32)


def pack_summary(*refs):
    *pieces, out_ref = refs
    for core in range(CORES):
        columns = slice(core * HALF, (core + 1) * HALF)
        for place, ref in enumerate(pieces):
            rows = slice(place * SUMMARY, (place + 1) * SUMMARY)
            for chip in range(CHIPS_Y):
                out_ref[chip * CORES + core, rows] = ref[:, columns]


def pack_other(place_ref, query_ref, key_ref, value_ref, out_ref):
    other = pl.multiple_of((1 - place_ref[2]) * HALF, HALF)
    for part, ref in enumerate((query_ref, key_ref, value_ref)):
        out_ref[part * ROWS : (part + 1) * ROWS] = ref[:, pl.ds(other, HALF)]


def slab_keys(slab, head):
    columns = slice(head * HEAD_DIM, (head + 1) * HEAD_DIM)
    sources = slab.shape[0]
    keys = slab[:, : 2 * SUMMARY, columns].reshape(sources * 2 * SUMMARY, HEAD_DIM)
    values = slab[:, 2 * SUMMARY :, columns].reshape(sources * 2 * SUMMARY, HEAD_DIM)
    return keys, values


def fold_slab(queries, state, slab, first_blocks):
    max_ref, sum_ref, acc_ref = state
    for virtual in range(VIRTUAL):
        keys, values = slab_keys(slab, virtual % 2)
        scores = rows_dot(keys, queries[virtual]) * SCALE
        if first_blocks is not None:
            shape = scores.shape
            key_block = lax.broadcasted_iota(jnp.int32, shape, 0) // SUMMARY
            query_block = first_blocks[virtual // 2] + lax.broadcasted_iota(jnp.int32, shape, 1) // BLOCK
            allowed = key_block < query_block
            scores = jnp.where(allowed, scores, MINUS)
        old_max = max_ref[virtual]
        new_max = jnp.maximum(old_max, jnp.max(scores, axis=0, keepdims=True))
        weights = jnp.exp2(scores - new_max)
        shrink = jnp.exp2(old_max - new_max)
        max_ref[virtual] = new_max
        sum_ref[virtual] = sum_ref[virtual] * shrink + jnp.sum(weights, axis=0, keepdims=True)
        acc_ref[virtual] = acc_ref[virtual] * shrink + columns_dot(values, weights.astype(BF16))


def band(query_ref, key_ref, value_ref, mine, other_ref, state, queries_ref):
    max_ref, sum_ref, acc_ref = state
    shape = (BLOCK, BLOCK)
    causal = lax.broadcasted_iota(jnp.int32, shape, 0) <= lax.broadcasted_iota(jnp.int32, shape, 1)
    for virtual in range(VIRTUAL):
        owner, head = divmod(virtual, 2)
        for block in range(2):
            rows = slice(block * BLOCK, (block + 1) * BLOCK)
            if owner == 0:
                columns = pl.ds(mine + head * HEAD_DIM, HEAD_DIM)
                query, key, value = (ref[rows, columns] for ref in (query_ref, key_ref, value_ref))
            else:
                columns = slice(head * HEAD_DIM, (head + 1) * HEAD_DIM)
                query, key, value = (
                    other_ref[part * ROWS + block * BLOCK : part * ROWS + (block + 1) * BLOCK, columns]
                    for part in range(3)
                )
            queries_ref[virtual, rows] = query
            scores = jnp.where(causal, rows_dot(key, query) * SCALE, MINUS)
            new_max = jnp.max(scores, axis=0, keepdims=True)
            weights = jnp.exp2(scores - new_max)
            max_ref[virtual, :, rows] = new_max
            sum_ref[virtual, :, rows] = jnp.sum(weights, axis=0, keepdims=True)
            acc_ref[virtual, :, rows] = columns_dot(value, weights.astype(BF16))


def finish(core, state, own_ref, other_ref, square_ref):
    _, sum_ref, acc_ref = state
    for owner, ref in enumerate((own_ref, other_ref)):
        total = jnp.zeros((1, ROWS), F32)
        for head in range(2):
            virtual = owner * 2 + head
            attended = acc_ref[virtual] / sum_ref[virtual]
            ref[head] = attended
            total += jnp.sum(attended * attended, axis=0, keepdims=True)
        square_ref[core if owner == 0 else 1 - core] = jnp.broadcast_to(total, square_ref.shape[1:])


def start_attention(place_ref, query_ref, key_ref, value_ref, other_in_ref, slab_ref, queries_ref, *state):
    chip, core = place_ref[1], place_ref[2]
    mine = pl.multiple_of(core * HALF, HALF)
    band(query_ref, key_ref, value_ref, mine, other_in_ref, state, queries_ref)
    first_blocks = [(chip * CORES + core) * 2, (chip * CORES + 1 - core) * 2]
    fold_slab(queries_ref, state, slab_ref, first_blocks)


def go_on(steps, place_ref, queries_ref, *refs):
    slabs, old_state, state = refs[: 2 * len(steps)], refs[2 * len(steps) : -3], refs[-3:]
    here = place_ref[0]
    for old_ref, ref in zip(old_state, state):
        ref[...] = old_ref[...]
    for turn, step in enumerate(steps):
        for slab, reached in zip(slabs[2 * turn : 2 * turn + 2], (here >= step, here + step >= CHIPS_Z)):

            @pl.when(reached)
            def _(slab=slab):
                fold_slab(queries_ref, state, slab, None)


def end_attention(steps, place_ref, queries_ref, *refs):
    inputs, outs, state = refs[:-6], refs[-6:-3], refs[-3:]
    go_on(steps, place_ref, queries_ref, *inputs, *state)
    finish(place_ref[2], state, *outs)


def scale_rows(place_ref, own_ref, other_ref, square_ref, gain_ref, out_ref):
    core = place_ref[2]
    total = jnp.sum(square_ref[...], axis=0, keepdims=True)
    scale = lax.rsqrt(total * (1.0 / FEATURES) + 1e-06)
    for owner, ref in enumerate((own_ref, other_ref)):
        first = pl.multiple_of((core if owner == 0 else 1 - core) * HALF, HALF)
        for head in range(2):
            columns = pl.ds(first + head * HEAD_DIM, HEAD_DIM)
            rows = jnp.transpose(ref[head] * scale)
            out_ref[:, columns] = (rows * gain_ref[:, columns]).astype(BF16)


def call(body, out_shape, in_specs, scratch=(), cost=None, **more):
    outs = jax.tree.map(lambda _: VMEM, out_shape)
    return pl.pallas_call(
        body,
        out_shape=out_shape,
        in_specs=in_specs,
        out_specs=outs,
        scratch_shapes=list(scratch),
        cost_estimate=cost,
        compiler_params=pltpu.CompilerParams(vmem_limit_bytes=LIMIT),
        **more,
    )


def groups(axes):
    made = {}
    for index in range(CHIPS_Z * SLAB):
        coordinate = {"z": index // SLAB, "y": index // CORES % CHIPS_Y, "c": index % CORES}
        made.setdefault(tuple(v for k, v in coordinate.items() if k not in axes), []).append(index)
    return list(made.values())


def swap_cores(array):
    pairs = [(index, index ^ 1) for index in range(CHIPS_Z * SLAB)]
    return lax.ppermute(array, "ctx", pairs)


def pass_on(array, step, way):
    pairs = []
    for index in range(CHIPS_Z * SLAB):
        here = index // SLAB
        there = here + way
        source = (there - way * step) % CHIPS_Z
        needed = there >= step if way == 1 else source < CHIPS_Z // 2
        if needed and there < CHIPS_Z:
            pairs.append((index, there % CHIPS_Z * SLAB + index % SLAB))
    return lax.ppermute(array, "ctx", pairs)


def cost_of(slabs):
    scores = VIRTUAL * ROWS * SLAB * 2 * SUMMARY * slabs
    return pl.CostEstimate(flops=4 * HEAD_DIM * scores, bytes_accessed=slabs * 2**21, transcendentals=scores)


def local(head_count, query_rows, key_rows, value_rows, out_gain):
    index = lax.axis_index("ctx")
    place = jnp.stack([index >> 3, (index >> 1) & (CHIPS_Y - 1), index & 1]).astype(jnp.int32)

    summary_rows = [pl.BlockSpec((SUMMARY, 2 * HALF), lambda _, block=block: (block, 0)) for block in (15, 31)]
    packed = pl.pallas_call(
        pack_summary,
        grid=(1,),
        out_shape=jax.ShapeDtypeStruct((SLAB, 4 * SUMMARY, HALF), BF16),
        in_specs=summary_rows * 2,
        out_specs=pl.BlockSpec((SLAB, 4 * SUMMARY, HALF), lambda _: (0, 0, 0)),
    )(key_rows, key_rows, value_rows, value_rows)
    slab = lax.all_to_all(packed, "ctx", 0, 0, axis_index_groups=groups("yc"), tiled=True)
    to_other = call(pack_other, jax.ShapeDtypeStruct((3 * ROWS, HALF), BF16), [SMEM] + [VMEM] * 3)(
        place, query_rows, key_rows, value_rows
    )
    from_other = swap_cores(to_other)
    up, down, arrived = slab, slab, []
    for step in range(1, 5):
        if step == 4:
            up, down = up[: SLAB // 2], down[SLAB // 2 :]
        up, down = pass_on(up, step, 1), pass_on(down, step, -1)
        arrived.append((up, down))

    state = (
        jax.ShapeDtypeStruct((VIRTUAL, 1, ROWS), F32),
        jax.ShapeDtypeStruct((VIRTUAL, 1, ROWS), F32),
        jax.ShapeDtypeStruct((VIRTUAL, HEAD_DIM, ROWS), F32),
    )
    queries, *now = call(
        start_attention,
        (jax.ShapeDtypeStruct((VIRTUAL, ROWS, HEAD_DIM), BF16), *state),
        [SMEM] + [VMEM] * 5,
        cost=cost_of(2),
    )(place, query_rows, key_rows, value_rows, from_other, slab)
    for steps in ((1, 2), (3,)):
        slabs = [part for step in steps for part in arrived[step - 1]]
        now = call(
            functools.partial(go_on, steps),
            state,
            [SMEM] + [VMEM] * (4 + len(slabs)),
            cost=cost_of(len(slabs)),
            input_output_aliases={2 + len(slabs) + i: i for i in range(3)},
        )(place, queries, *slabs, *now)
    attended = jax.ShapeDtypeStruct((2, HEAD_DIM, ROWS), F32)
    own, other, squares = call(
        functools.partial(end_attention, (4,)),
        (attended, attended, jax.ShapeDtypeStruct((CORES, head_count, ROWS), F32)),
        [SMEM] + [VMEM] * 6,
        scratch=[pltpu.VMEM(part.shape, F32) for part in state],
    )(place, queries, *arrived[3], *now)
    back = swap_cores(other)
    chips = [
        [(chip * CORES + core) * head_count + head for core in range(CORES) for head in range(head_count)]
        for chip in range(CHIPS_Z * CHIPS_Y)
    ]
    totals = lax.all_to_all(
        squares.reshape(CORES * head_count, ROWS), ("ctx", "head"), 0, 0, axis_index_groups=chips, tiled=True
    )
    return call(scale_rows, jax.ShapeDtypeStruct((ROWS, 4 * HEAD_DIM), BF16), [SMEM] + [VMEM] * 4)(
        place, own, back, totals, out_gain[None]
    )


def solution(mesh):
    placed = (P("ctx", "head"), P("ctx", "head"), P("ctx", "head"), P("head"))
    return jax.shard_map(
        functools.partial(local, mesh.shape["head"]),
        mesh=mesh,
        in_specs=placed,
        out_specs=P("ctx", "head"),
        check_vma=False,
    )
```

```python
import functools
import math

import jax
import jax.numpy as jnp
from jax import lax
from jax.experimental import pallas as pl
from jax.experimental.pallas import tpu as pltpu
from jax.sharding import PartitionSpec as P

HEAD_DIM = 128
BLOCK = 256
SUMMARY = 16
FEATURES = 4096
CHIPS_Z, CHIPS_Y, CORES = 8, 4, 2
SLAB = CHIPS_Y * CORES
HALF = 256
ROWS = 512
SCALE = HEAD_DIM**-0.5 * math.log2(math.e)
MINUS = -1e30
VIRTUAL = 4
VMEM = pl.BlockSpec(memory_space=pltpu.VMEM)
SMEM = pl.BlockSpec(memory_space=pltpu.SMEM)
LIMIT = 24 * 1024 * 1024

F32 = jnp.float32
BF16 = jnp.bfloat16


def rows_dot(a, b):
    return lax.dot_general(a, b, (((1,), (1,)), ((), ())), preferred_element_type=F32)


def columns_dot(a, b):
    return lax.dot_general(a, b, (((0,), (0,)), ((), ())), preferred_element_type=F32)


def pack_summary(*refs):
    *pieces, out_ref = refs
    for core in range(CORES):
        columns = slice(core * HALF, (core + 1) * HALF)
        for place, ref in enumerate(pieces):
            rows = slice(place * SUMMARY, (place + 1) * SUMMARY)
            for chip in range(CHIPS_Y):
                out_ref[chip * CORES + core, rows] = ref[:, columns]


def pack_other(place_ref, query_ref, key_ref, value_ref, out_ref):
    other = pl.multiple_of((1 - place_ref[2]) * HALF, HALF)
    for part, ref in enumerate((query_ref, key_ref, value_ref)):
        out_ref[part * ROWS : (part + 1) * ROWS] = ref[:, pl.ds(other, HALF)]


def slab_keys(slab, head):
    columns = slice(head * HEAD_DIM, (head + 1) * HEAD_DIM)
    sources = slab.shape[0]
    keys = slab[:, : 2 * SUMMARY, columns].reshape(sources * 2 * SUMMARY, HEAD_DIM)
    values = slab[:, 2 * SUMMARY :, columns].reshape(sources * 2 * SUMMARY, HEAD_DIM)
    return keys, values


def fold_slab(queries, state, slab, first_blocks):
    max_ref, sum_ref, acc_ref = state
    parts = [slab_keys(slab, head) for head in range(2)]
    staged = []
    for virtual in range(VIRTUAL):
        scores = rows_dot(parts[virtual % 2][0], queries[virtual]) * SCALE
        if first_blocks is not None:
            shape = scores.shape
            key_block = lax.broadcasted_iota(jnp.int32, shape, 0) // SUMMARY
            query_block = first_blocks[virtual // 2] + lax.broadcasted_iota(jnp.int32, shape, 1) // BLOCK
            scores = jnp.where(key_block < query_block, scores, MINUS)
        old_max = max_ref[virtual]
        new_max = jnp.maximum(old_max, jnp.max(scores, axis=0, keepdims=True))
        staged.append((jnp.exp2(scores - new_max), jnp.exp2(old_max - new_max)))
        max_ref[virtual] = new_max
    for virtual, (weights, shrink) in enumerate(staged):
        sum_ref[virtual] = sum_ref[virtual] * shrink + jnp.sum(weights, axis=0, keepdims=True)
        acc_ref[virtual] = acc_ref[virtual] * shrink + columns_dot(parts[virtual % 2][1], weights.astype(BF16))


def band(pieces, first, state, queries_ref):
    max_ref, sum_ref, acc_ref = state
    shape = (BLOCK, BLOCK)
    causal = lax.broadcasted_iota(jnp.int32, shape, 0) <= lax.broadcasted_iota(jnp.int32, shape, 1)
    staged = []
    for head in range(2):
        for block in range(2):
            virtual, rows = first + head, slice(block * BLOCK, (block + 1) * BLOCK)
            query, key, value = pieces(head, block)
            queries_ref[virtual, rows] = query
            scores = jnp.where(causal, rows_dot(key, query) * SCALE, MINUS)
            new_max = jnp.max(scores, axis=0, keepdims=True)
            max_ref[virtual, :, rows] = new_max
            staged.append((virtual, rows, value, jnp.exp2(scores - new_max)))
    for virtual, rows, value, weights in staged:
        sum_ref[virtual, :, rows] = jnp.sum(weights, axis=0, keepdims=True)
        acc_ref[virtual, :, rows] = columns_dot(value, weights.astype(BF16))


def finish(core, gain_ref, state, own_ref, other_ref, square_ref):
    _, sum_ref, acc_ref = state
    mine = pl.multiple_of(core * HALF, HALF)
    for owner, ref in enumerate((own_ref, other_ref)):
        total = jnp.zeros((1, ROWS), F32)
        for head in range(2):
            virtual = owner * 2 + head
            gain = jnp.broadcast_to(gain_ref[:, pl.ds(mine + head * HEAD_DIM, HEAD_DIM)], (8, HEAD_DIM))
            attended = acc_ref[virtual] * (1.0 / sum_ref[virtual])
            ref[head] = attended * jnp.transpose(gain)[:, :1]
            total += jnp.sum(attended * attended, axis=0, keepdims=True)
        square_ref[core if owner == 0 else 1 - core] = jnp.broadcast_to(total, square_ref.shape[1:])


def start_attention(place_ref, query_ref, key_ref, value_ref, queries_ref, *state):
    mine = pl.multiple_of(place_ref[2] * HALF, HALF)

    def pieces(head, block):
        rows, columns = slice(block * BLOCK, (block + 1) * BLOCK), pl.ds(mine + head * HEAD_DIM, HEAD_DIM)
        return (ref[rows, columns] for ref in (query_ref, key_ref, value_ref))

    band(pieces, 0, state, queries_ref)


def own_slab(place_ref, other_in_ref, slab_ref, *refs):
    inputs, outs = refs[:4], refs[4:]
    queries_ref, *state = outs
    for ref_in, ref in zip(inputs, outs):
        ref[:2] = ref_in[...]

    def pieces(head, block):
        columns = slice(head * HEAD_DIM, (head + 1) * HEAD_DIM)
        starts = [part * ROWS + block * BLOCK for part in range(3)]
        return (other_in_ref[start : start + BLOCK, columns] for start in starts)

    band(pieces, 2, state, queries_ref)
    chip, core = place_ref[1], place_ref[2]
    first_blocks = [(chip * CORES + core) * 2, (chip * CORES + 1 - core) * 2]
    fold_slab(queries_ref, state, slab_ref, first_blocks)


def go_on(steps, place_ref, queries_ref, *refs):
    slabs, old_state, state = refs[: 2 * len(steps)], refs[2 * len(steps) : -3], refs[-3:]
    here = place_ref[0]
    for old_ref, ref in zip(old_state, state):
        ref[...] = old_ref[...]
    for turn, step in enumerate(steps):
        for slab, reached in zip(slabs[2 * turn : 2 * turn + 2], (here >= step, here + step >= CHIPS_Z)):

            @pl.when(reached)
            def _(slab=slab):
                fold_slab(queries_ref, state, slab, None)


def end_attention(steps, place_ref, gain_ref, queries_ref, *refs):
    inputs, outs, state = refs[:-6], refs[-6:-3], refs[-3:]
    go_on(steps, place_ref, queries_ref, *inputs, *state)
    finish(place_ref[2], gain_ref, state, *outs)


def scale_rows(place_ref, own_ref, other_ref, square_ref, out_ref):
    core = place_ref[2]
    total = jnp.sum(square_ref[...], axis=0, keepdims=True)
    scale = lax.rsqrt(total * (1.0 / FEATURES) + 1e-06)
    for owner, ref in enumerate((own_ref, other_ref)):
        first = pl.multiple_of((core if owner == 0 else 1 - core) * HALF, HALF)
        for head in range(2):
            columns = pl.ds(first + head * HEAD_DIM, HEAD_DIM)
            out_ref[:, columns] = jnp.transpose(ref[head] * scale).astype(BF16)


def call(body, out_shape, in_specs, scratch=(), cost=None, **more):
    outs = jax.tree.map(lambda _: VMEM, out_shape)
    return pl.pallas_call(
        body,
        out_shape=out_shape,
        in_specs=in_specs,
        out_specs=outs,
        scratch_shapes=list(scratch),
        cost_estimate=cost,
        compiler_params=pltpu.CompilerParams(vmem_limit_bytes=LIMIT),
        **more,
    )


def groups(axes):
    made = {}
    for index in range(CHIPS_Z * SLAB):
        coordinate = {"z": index // SLAB, "y": index // CORES % CHIPS_Y, "c": index % CORES}
        made.setdefault(tuple(v for k, v in coordinate.items() if k not in axes), []).append(index)
    return list(made.values())


def swap_cores(array):
    pairs = [(index, index ^ 1) for index in range(CHIPS_Z * SLAB)]
    return lax.ppermute(array, "ctx", pairs)


def pass_on(array, step, way):
    pairs = []
    for index in range(CHIPS_Z * SLAB):
        here = index // SLAB
        there = here + way
        source = (there - way * step) % CHIPS_Z
        needed = there >= step if way == 1 else source < CHIPS_Z // 2
        if needed and there < CHIPS_Z:
            pairs.append((index, there % CHIPS_Z * SLAB + index % SLAB))
    return lax.ppermute(array, "ctx", pairs)


FIRST_COST = pl.CostEstimate(flops=3 * 10**10, bytes_accessed=2**20, transcendentals=2**20)
COST = pl.CostEstimate(flops=3 * 10**9, bytes_accessed=2**20, transcendentals=2**20)


def local(head_count, query_rows, key_rows, value_rows, out_gain):
    index = lax.axis_index("ctx")
    place = jnp.stack([index >> 3, (index >> 1) & (CHIPS_Y - 1), index & 1]).astype(jnp.int32)

    summary_rows = [pl.BlockSpec((SUMMARY, 2 * HALF), lambda _, block=block: (block, 0)) for block in (15, 31)]
    packed = pl.pallas_call(
        pack_summary,
        grid=(1,),
        out_shape=jax.ShapeDtypeStruct((SLAB, 4 * SUMMARY, HALF), BF16),
        in_specs=summary_rows * 2,
        out_specs=pl.BlockSpec((SLAB, 4 * SUMMARY, HALF), lambda _: (0, 0, 0)),
    )(key_rows, key_rows, value_rows, value_rows)
    slab = lax.all_to_all(packed, "ctx", 0, 0, axis_index_groups=groups("yc"), tiled=True)
    query_rows, key_rows, value_rows, _ = lax.optimization_barrier((query_rows, key_rows, value_rows, packed))
    to_other = call(pack_other, jax.ShapeDtypeStruct((3 * ROWS, HALF), BF16), [SMEM] + [VMEM] * 3)(
        place, query_rows, key_rows, value_rows
    )
    from_other = swap_cores(to_other)

    def attention(virtuals):
        return (
            jax.ShapeDtypeStruct((virtuals, ROWS, HEAD_DIM), BF16),
            jax.ShapeDtypeStruct((virtuals, 1, ROWS), F32),
            jax.ShapeDtypeStruct((virtuals, 1, ROWS), F32),
            jax.ShapeDtypeStruct((virtuals, HEAD_DIM, ROWS), F32),
        )

    mine = call(start_attention, attention(2), [SMEM] + [VMEM] * 3, cost=FIRST_COST)(place, query_rows, key_rows, value_rows)
    state = attention(VIRTUAL)[1:]
    up, down, arrived = slab, slab, []
    for step in range(1, 5):
        if step == 1:
            up, down, mine = lax.optimization_barrier((up, down, mine))
        else:
            up, now = lax.optimization_barrier((up, now))
            down, now = lax.optimization_barrier((down, now))
        if step == 4:
            up, down = up[: SLAB // 2], down[SLAB // 2 :]
        up, down = pass_on(up, step, 1), pass_on(down, step, -1)
        if step == 1:
            queries, *now = call(own_slab, attention(VIRTUAL), [SMEM] + [VMEM] * 6, cost=COST)(place, from_other, slab, *mine)
        else:
            now = call(
                functools.partial(go_on, (step - 1,)),
                state,
                [SMEM] + [VMEM] * 6,
                cost=COST,
                input_output_aliases={4 + i: i for i in range(3)},
            )(place, queries, *arrived[-1], *now)
        arrived.append((up, down))
    attended = jax.ShapeDtypeStruct((2, HEAD_DIM, ROWS), F32)
    own, other, squares = call(
        functools.partial(end_attention, (4,)),
        (attended, attended, jax.ShapeDtypeStruct((CORES, head_count, ROWS), F32)),
        [SMEM] + [VMEM] * 7,
        scratch=[pltpu.VMEM(part.shape, F32) for part in state],
    )(place, out_gain[None], queries, *arrived[3], *now)
    back = swap_cores(other)
    chips = [
        [(chip * CORES + core) * head_count + head for core in range(CORES) for head in range(head_count)]
        for chip in range(CHIPS_Z * CHIPS_Y)
    ]
    totals = lax.all_to_all(
        squares.reshape(CORES * head_count, ROWS), ("ctx", "head"), 0, 0, axis_index_groups=chips, tiled=True
    )
    return call(scale_rows, jax.ShapeDtypeStruct((ROWS, 4 * HEAD_DIM), BF16), [SMEM] + [VMEM] * 3)(
        place, own, back, totals
    )


def solution(mesh):
    placed = (P("ctx", "head"), P("ctx", "head"), P("ctx", "head"), P("head"))
    return jax.shard_map(
        functools.partial(local, mesh.shape["head"]),
        mesh=mesh,
        in_specs=placed,
        out_specs=P("ctx", "head"),
        check_vma=False,
    )
```

```python
import functools
import math

import jax
import jax.numpy as jnp
from jax import lax
from jax.experimental import pallas as pl
from jax.experimental.pallas import tpu as pltpu
from jax.sharding import PartitionSpec as P

HEAD_DIM = 128
BLOCK = 256
SUMMARY = 16
FEATURES = 4096
CHIPS_Z, CHIPS_Y, CORES = 8, 4, 2
SLAB = CHIPS_Y * CORES
HALF = 256
ROWS = 512
SCALE = HEAD_DIM**-0.5 * math.log2(math.e)
MINUS = -1e30
VIRTUAL = 4
VMEM = pl.BlockSpec(memory_space=pltpu.VMEM)
SMEM = pl.BlockSpec(memory_space=pltpu.SMEM)
LIMIT = 24 * 1024 * 1024

F32 = jnp.float32
BF16 = jnp.bfloat16


def rows_dot(a, b):
    return lax.dot_general(a, b, (((1,), (1,)), ((), ())), preferred_element_type=F32)


def columns_dot(a, b):
    return lax.dot_general(a, b, (((0,), (0,)), ((), ())), preferred_element_type=F32)


def pack_summary(*refs):
    *pieces, out_ref = refs
    for core in range(CORES):
        columns = slice(core * HALF, (core + 1) * HALF)
        for place, ref in enumerate(pieces):
            rows = slice(place * SUMMARY, (place + 1) * SUMMARY)
            for chip in range(CHIPS_Y):
                out_ref[chip * CORES + core, rows] = ref[:, columns]


def pack_other(place_ref, query_ref, key_ref, value_ref, out_ref):
    other = pl.multiple_of((1 - place_ref[2]) * HALF, HALF)
    for part, ref in enumerate((query_ref, key_ref, value_ref)):
        out_ref[part * ROWS : (part + 1) * ROWS] = ref[:, pl.ds(other, HALF)]


def slab_keys(slabs, head):
    columns = slice(head * HEAD_DIM, (head + 1) * HEAD_DIM)

    def joined(rows):
        return jnp.concatenate([slab[:, rows, columns].reshape(-1, HEAD_DIM) for slab in slabs])

    return joined(slice(0, 2 * SUMMARY)), joined(slice(2 * SUMMARY, 4 * SUMMARY))


def fold_slab(queries, state, slabs, first_blocks):
    max_ref, sum_ref, acc_ref = state
    parts = [slab_keys(slabs, head) for head in range(2)]
    staged = []
    for virtual in range(VIRTUAL):
        scores = rows_dot(parts[virtual % 2][0], queries[virtual]) * SCALE
        if first_blocks is not None:
            shape = scores.shape
            key_block = lax.broadcasted_iota(jnp.int32, shape, 0) // SUMMARY
            query_block = first_blocks[virtual // 2] + lax.broadcasted_iota(jnp.int32, shape, 1) // BLOCK
            scores = jnp.where(key_block < query_block, scores, MINUS)
        old_max = max_ref[virtual]
        new_max = jnp.maximum(old_max, jnp.max(scores, axis=0, keepdims=True))
        staged.append((jnp.exp2(scores - new_max), jnp.exp2(old_max - new_max)))
        max_ref[virtual] = new_max
    for virtual, (weights, shrink) in enumerate(staged):
        sum_ref[virtual] = sum_ref[virtual] * shrink + jnp.sum(weights, axis=0, keepdims=True)
        acc_ref[virtual] = acc_ref[virtual] * shrink + columns_dot(parts[virtual % 2][1], weights.astype(BF16))


def band(pieces, first, state, queries_ref):
    max_ref, sum_ref, acc_ref = state
    shape = (BLOCK, BLOCK)
    causal = lax.broadcasted_iota(jnp.int32, shape, 0) <= lax.broadcasted_iota(jnp.int32, shape, 1)
    staged = []
    for head in range(2):
        for block in range(2):
            virtual, rows = first + head, slice(block * BLOCK, (block + 1) * BLOCK)
            query, key, value = pieces(head, block)
            queries_ref[virtual, rows] = query
            scores = jnp.where(causal, rows_dot(key, query) * SCALE, MINUS)
            new_max = jnp.max(scores, axis=0, keepdims=True)
            max_ref[virtual, :, rows] = new_max
            staged.append((virtual, rows, value, jnp.exp2(scores - new_max)))
    for virtual, rows, value, weights in staged:
        sum_ref[virtual, :, rows] = jnp.sum(weights, axis=0, keepdims=True)
        acc_ref[virtual, :, rows] = columns_dot(value, weights.astype(BF16))


def gain_columns(place_ref, gain_ref, out_ref):
    mine = pl.multiple_of(place_ref[2] * HALF, HALF)
    for head in range(2):
        gain = gain_ref[:, pl.ds(mine + head * HEAD_DIM, HEAD_DIM)]
        out_ref[head] = jnp.transpose(jnp.broadcast_to(gain, (8, HEAD_DIM)))


def finish(core, gain_ref, state, own_ref, other_ref, square_ref):
    _, sum_ref, acc_ref = state
    for owner, ref in enumerate((own_ref, other_ref)):
        total = jnp.zeros((1, ROWS), F32)
        for head in range(2):
            virtual = owner * 2 + head
            attended = acc_ref[virtual] * (1.0 / sum_ref[virtual])
            ref[head] = attended * gain_ref[head, :, :1]
            total += jnp.sum(attended * attended, axis=0, keepdims=True)
        square_ref[core if owner == 0 else 1 - core] = jnp.broadcast_to(total, square_ref.shape[1:])


def start_attention(place_ref, query_ref, key_ref, value_ref, other_in_ref, slab_ref, queries_ref, *state):
    mine = pl.multiple_of(place_ref[2] * HALF, HALF)

    def own_pieces(head, block):
        rows, columns = slice(block * BLOCK, (block + 1) * BLOCK), pl.ds(mine + head * HEAD_DIM, HEAD_DIM)
        return (ref[rows, columns] for ref in (query_ref, key_ref, value_ref))

    def other_pieces(head, block):
        columns = slice(head * HEAD_DIM, (head + 1) * HEAD_DIM)
        starts = [part * ROWS + block * BLOCK for part in range(3)]
        return (other_in_ref[start : start + BLOCK, columns] for start in starts)

    band(own_pieces, 0, state, queries_ref)
    band(other_pieces, 2, state, queries_ref)
    chip, core = place_ref[1], place_ref[2]
    first_blocks = [(chip * CORES + core) * 2, (chip * CORES + 1 - core) * 2]
    fold_slab(queries_ref, state, [slab_ref], first_blocks)


def go_on(step, place_ref, queries_ref, up_ref, down_ref, *refs):
    old_state, state = refs[:3], refs[3:]
    here = place_ref[0]
    for old_ref, ref in zip(old_state, state):
        ref[...] = old_ref[...]
    below, above = here >= step, here + step >= CHIPS_Z
    if step == 4:
        cases = ((below, [up_ref, down_ref]),)
    elif step == 1:
        cases = ((below & ~above, [up_ref]), (below & above, [up_ref, down_ref]))
    else:
        cases = ((below & ~above, [up_ref]), (above & ~below, [down_ref]), (below & above, [up_ref, down_ref]))
    for reached, slabs in cases:

        @pl.when(reached)
        def _(slabs=slabs):
            fold_slab(queries_ref, state, slabs, None)


def end_attention(step, place_ref, gain_ref, queries_ref, up_ref, down_ref, *refs):
    old_state, outs, state = refs[:3], refs[3:6], refs[6:]
    go_on(step, place_ref, queries_ref, up_ref, down_ref, *old_state, *state)
    finish(place_ref[2], gain_ref, state, *outs)


def scale_rows(place_ref, own_ref, other_ref, square_ref, out_ref):
    core = place_ref[2]
    total = jnp.sum(square_ref[...], axis=0, keepdims=True)
    scale = lax.rsqrt(total * (1.0 / FEATURES) + 1e-06)
    for owner, ref in enumerate((own_ref, other_ref)):
        first = pl.multiple_of((core if owner == 0 else 1 - core) * HALF, HALF)
        for head in range(2):
            columns = pl.ds(first + head * HEAD_DIM, HEAD_DIM)
            out_ref[:, columns] = jnp.transpose(ref[head] * scale).astype(BF16)


def call(body, out_shape, in_specs, scratch=(), cost=None, **more):
    outs = jax.tree.map(lambda _: VMEM, out_shape)
    return pl.pallas_call(
        body,
        out_shape=out_shape,
        in_specs=in_specs,
        out_specs=outs,
        scratch_shapes=list(scratch),
        cost_estimate=cost,
        compiler_params=pltpu.CompilerParams(vmem_limit_bytes=LIMIT),
        **more,
    )


def groups(axes):
    made = {}
    for index in range(CHIPS_Z * SLAB):
        coordinate = {"z": index // SLAB, "y": index // CORES % CHIPS_Y, "c": index % CORES}
        made.setdefault(tuple(v for k, v in coordinate.items() if k not in axes), []).append(index)
    return list(made.values())


def swap_cores(array):
    pairs = [(index, index ^ 1) for index in range(CHIPS_Z * SLAB)]
    return lax.ppermute(array, "ctx", pairs)


def pass_on(array, step, way):
    pairs = []
    for index in range(CHIPS_Z * SLAB):
        there = index // SLAB + way
        source = (there - way * step) % CHIPS_Z
        needed = there >= step if way == 1 else source < CHIPS_Z // 2
        if needed and there < CHIPS_Z:
            pairs.append((index, there % CHIPS_Z * SLAB + index % SLAB))
    return lax.ppermute(array, "ctx", pairs)


LONG = pl.CostEstimate(flops=3 * 10**10, bytes_accessed=2**20, transcendentals=0)
COST = pl.CostEstimate(flops=3 * 10**9, bytes_accessed=2**20, transcendentals=2**20)


def local(head_count, query_rows, key_rows, value_rows, out_gain):
    index = lax.axis_index("ctx")
    place = jnp.stack([index >> 3, (index >> 1) & (CHIPS_Y - 1), index & 1]).astype(jnp.int32)

    summary_rows = [pl.BlockSpec((SUMMARY, 2 * HALF), lambda _, block=block: (block, 0)) for block in (15, 31)]
    packed = pl.pallas_call(
        pack_summary,
        grid=(1,),
        out_shape=jax.ShapeDtypeStruct((SLAB, 4 * SUMMARY, HALF), BF16),
        in_specs=summary_rows * 2,
        out_specs=pl.BlockSpec((SLAB, 4 * SUMMARY, HALF), lambda _: (0, 0, 0)),
    )(key_rows, key_rows, value_rows, value_rows)
    slab = lax.all_to_all(packed, "ctx", 0, 0, axis_index_groups=groups("yc"), tiled=True)
    query_rows, key_rows, value_rows, _ = lax.optimization_barrier((query_rows, key_rows, value_rows, packed))
    to_other = call(pack_other, jax.ShapeDtypeStruct((3 * ROWS, HALF), BF16), [SMEM] + [VMEM] * 3)(
        place, query_rows, key_rows, value_rows
    )
    from_other = swap_cores(to_other)
    gain = call(gain_columns, jax.ShapeDtypeStruct((2, HEAD_DIM, 8), F32), [SMEM, VMEM], cost=LONG)(place, out_gain[None])

    def attention(virtuals):
        return (
            jax.ShapeDtypeStruct((virtuals, ROWS, HEAD_DIM), BF16),
            jax.ShapeDtypeStruct((virtuals, 1, ROWS), F32),
            jax.ShapeDtypeStruct((virtuals, 1, ROWS), F32),
            jax.ShapeDtypeStruct((virtuals, HEAD_DIM, ROWS), F32),
        )

    state = attention(VIRTUAL)[1:]
    up, down, arrived = slab, slab, []
    for step in range(1, 5):
        if step == 1:
            up, down, gain = lax.optimization_barrier((up, down, gain))
        else:
            up, now = lax.optimization_barrier((up, now))
        if step == 4:
            up, down = up[: SLAB // 2], down[SLAB // 2 :]
        up, down = pass_on(up, step, 1), pass_on(down, step, -1)
        if step == 1:
            queries, *now = call(start_attention, attention(VIRTUAL), [SMEM] + [VMEM] * 5, cost=COST)(
                place, query_rows, key_rows, value_rows, from_other, slab
            )
        else:
            now = call(
                functools.partial(go_on, step - 1),
                state,
                [SMEM] + [VMEM] * 6,
                cost=COST,
                input_output_aliases={4 + i: i for i in range(3)},
            )(place, queries, *arrived[-1], *now)
        arrived.append((up, down))
    attended = jax.ShapeDtypeStruct((2, HEAD_DIM, ROWS), F32)
    own, other, squares = call(
        functools.partial(end_attention, 4),
        (attended, attended, jax.ShapeDtypeStruct((CORES, head_count, ROWS), F32)),
        [SMEM] + [VMEM] * 7,
        scratch=[pltpu.VMEM(part.shape, F32) for part in state],
    )(place, gain, queries, *arrived[3], *now)
    back = swap_cores(other)
    chips = [
        [(chip * CORES + core) * head_count + head for core in range(CORES) for head in range(head_count)]
        for chip in range(CHIPS_Z * CHIPS_Y)
    ]
    totals = lax.all_to_all(
        squares.reshape(CORES * head_count, ROWS), ("ctx", "head"), 0, 0, axis_index_groups=chips, tiled=True
    )
    return call(scale_rows, jax.ShapeDtypeStruct((ROWS, 4 * HEAD_DIM), BF16), [SMEM] + [VMEM] * 3)(
        place, own, back, totals
    )


def solution(mesh):
    placed = (P("ctx", "head"), P("ctx", "head"), P("ctx", "head"), P("head"))
    return jax.shard_map(
        functools.partial(local, mesh.shape["head"]),
        mesh=mesh,
        in_specs=placed,
        out_specs=P("ctx", "head"),
        check_vma=False,
    )
```

```python
import functools
import math

import jax
import jax.numpy as jnp
from jax import lax
from jax.experimental import pallas as pl
from jax.experimental.pallas import tpu as pltpu
from jax.sharding import PartitionSpec as P

HEAD_DIM = 128
BLOCK = 256
SUMMARY = 16
FEATURES = 4096
CHIPS_Z, CHIPS_Y, CORES = 8, 4, 2
SLAB = CHIPS_Y * CORES
HALF = 256
ROWS = 512
SCALE = HEAD_DIM**-0.5 * math.log2(math.e)
MINUS = -1e30
VIRTUAL = 4
VMEM = pl.BlockSpec(memory_space=pltpu.VMEM)
SMEM = pl.BlockSpec(memory_space=pltpu.SMEM)
LIMIT = 24 * 1024 * 1024

F32 = jnp.float32
BF16 = jnp.bfloat16


def rows_dot(a, b):
    return lax.dot_general(a, b, (((1,), (1,)), ((), ())), preferred_element_type=F32)


def columns_dot(a, b):
    return lax.dot_general(a, b, (((0,), (0,)), ((), ())), preferred_element_type=F32)


def pack_summary(*refs):
    *pieces, out_ref = refs
    for core in range(CORES):
        columns = slice(core * HALF, (core + 1) * HALF)
        for place, ref in enumerate(pieces):
            rows = slice(place * SUMMARY, (place + 1) * SUMMARY)
            for chip in range(CHIPS_Y):
                out_ref[chip * CORES + core, rows] = ref[:, columns]


def pack_other(place_ref, query_ref, key_ref, value_ref, out_ref):
    other = pl.multiple_of((1 - place_ref[2]) * HALF, HALF)
    for part, ref in enumerate((query_ref, key_ref, value_ref)):
        out_ref[part * ROWS : (part + 1) * ROWS] = ref[:, pl.ds(other, HALF)]


def slab_keys(slabs, head):
    columns = slice(head * HEAD_DIM, (head + 1) * HEAD_DIM)

    def joined(rows):
        return jnp.concatenate([slab[:, rows, columns].reshape(-1, HEAD_DIM) for slab in slabs])

    return joined(slice(0, 2 * SUMMARY)), joined(slice(2 * SUMMARY, 4 * SUMMARY))


def fold_slab(queries, state, slabs, first_blocks):
    max_ref, sum_ref, acc_ref = state
    parts = [slab_keys(slabs, head) for head in range(2)]
    staged = []
    for virtual in range(VIRTUAL):
        scores = rows_dot(parts[virtual % 2][0], queries[virtual]) * SCALE
        if first_blocks is not None:
            shape = scores.shape
            key_block = lax.broadcasted_iota(jnp.int32, shape, 0) // SUMMARY
            query_block = first_blocks[virtual // 2] + lax.broadcasted_iota(jnp.int32, shape, 1) // BLOCK
            scores = jnp.where(key_block < query_block, scores, MINUS)
        old_max = max_ref[virtual]
        new_max = jnp.maximum(old_max, jnp.max(scores, axis=0, keepdims=True))
        staged.append((jnp.exp2(scores - new_max), jnp.exp2(old_max - new_max)))
        max_ref[virtual] = new_max
    for virtual, (weights, shrink) in enumerate(staged):
        sum_ref[virtual] = sum_ref[virtual] * shrink + jnp.sum(weights, axis=0, keepdims=True)
        acc_ref[virtual] = acc_ref[virtual] * shrink + columns_dot(parts[virtual % 2][1], weights.astype(BF16))


def band(pieces, first, state, queries_ref):
    max_ref, sum_ref, acc_ref = state
    shape = (BLOCK, BLOCK)
    causal = lax.broadcasted_iota(jnp.int32, shape, 0) <= lax.broadcasted_iota(jnp.int32, shape, 1)
    staged = []
    for head in range(2):
        for block in range(2):
            virtual, rows = first + head, slice(block * BLOCK, (block + 1) * BLOCK)
            query, key, value = pieces(head, block)
            queries_ref[virtual, rows] = query
            scores = jnp.where(causal, rows_dot(key, query) * SCALE, MINUS)
            new_max = jnp.max(scores, axis=0, keepdims=True)
            max_ref[virtual, :, rows] = new_max
            staged.append((virtual, rows, value, jnp.exp2(scores - new_max)))
    for virtual, rows, value, weights in staged:
        sum_ref[virtual, :, rows] = jnp.sum(weights, axis=0, keepdims=True)
        acc_ref[virtual, :, rows] = columns_dot(value, weights.astype(BF16))


def gain_columns(place_ref, gain_ref, out_ref):
    mine = pl.multiple_of(place_ref[2] * HALF, HALF)
    for head in range(2):
        gain = gain_ref[:, pl.ds(mine + head * HEAD_DIM, HEAD_DIM)]
        out_ref[head] = jnp.transpose(jnp.broadcast_to(gain, (8, HEAD_DIM)))


def finish(core, gain_ref, state, own_ref, other_ref, square_ref):
    _, sum_ref, acc_ref = state
    for owner, ref in enumerate((own_ref, other_ref)):
        total = jnp.zeros((1, ROWS), F32)
        for head in range(2):
            virtual = owner * 2 + head
            attended = acc_ref[virtual] * (1.0 / sum_ref[virtual])
            ref[head] = attended * gain_ref[head, :, :1]
            total += jnp.sum(attended * attended, axis=0, keepdims=True)
        square_ref[core if owner == 0 else 1 - core] = jnp.broadcast_to(total, square_ref.shape[1:])


def start_attention(place_ref, query_ref, key_ref, value_ref, other_in_ref, slab_ref, queries_ref, *state):
    mine = pl.multiple_of(place_ref[2] * HALF, HALF)

    def own_pieces(head, block):
        rows, columns = slice(block * BLOCK, (block + 1) * BLOCK), pl.ds(mine + head * HEAD_DIM, HEAD_DIM)
        return (ref[rows, columns] for ref in (query_ref, key_ref, value_ref))

    def other_pieces(head, block):
        columns = slice(head * HEAD_DIM, (head + 1) * HEAD_DIM)
        starts = [part * ROWS + block * BLOCK for part in range(3)]
        return (other_in_ref[start : start + BLOCK, columns] for start in starts)

    band(own_pieces, 0, state, queries_ref)
    band(other_pieces, 2, state, queries_ref)
    chip, core = place_ref[1], place_ref[2]
    first_blocks = [(chip * CORES + core) * 2, (chip * CORES + 1 - core) * 2]
    fold_slab(queries_ref, state, [slab_ref], first_blocks)


def go_on(step, place_ref, queries_ref, up_ref, down_ref, *refs):
    old_state, state = refs[:3], refs[3:]
    here = place_ref[0]
    for old_ref, ref in zip(old_state, state):
        ref[...] = old_ref[...]
    below, above = here >= step, here + step >= CHIPS_Z
    if step == 4:
        cases = ((below, [up_ref]),)
    elif step == 1:
        cases = ((below & ~above, [up_ref]), (below & above, [up_ref, down_ref]))
    else:
        cases = ((below & ~above, [up_ref]), (above & ~below, [down_ref]), (below & above, [up_ref, down_ref]))
    for reached, slabs in cases:

        @pl.when(reached)
        def _(slabs=slabs):
            fold_slab(queries_ref, state, slabs, None)


def end_attention(step, place_ref, gain_ref, queries_ref, up_ref, down_ref, *refs):
    old_state, outs, state = refs[:3], refs[3:6], refs[6:]
    go_on(step, place_ref, queries_ref, up_ref, down_ref, *old_state, *state)
    finish(place_ref[2], gain_ref, state, *outs)


def scale_rows(place_ref, own_ref, other_ref, square_ref, out_ref):
    core = place_ref[2]
    total = jnp.sum(square_ref[...], axis=0, keepdims=True)
    scale = lax.rsqrt(total * (1.0 / FEATURES) + 1e-06)
    for owner, ref in enumerate((own_ref, other_ref)):
        first = pl.multiple_of((core if owner == 0 else 1 - core) * HALF, HALF)
        for head in range(2):
            columns = pl.ds(first + head * HEAD_DIM, HEAD_DIM)
            out_ref[:, columns] = jnp.transpose(ref[head] * scale).astype(BF16)


def call(body, out_shape, in_specs, scratch=(), cost=None, **more):
    outs = jax.tree.map(lambda _: VMEM, out_shape)
    return pl.pallas_call(
        body,
        out_shape=out_shape,
        in_specs=in_specs,
        out_specs=outs,
        scratch_shapes=list(scratch),
        cost_estimate=cost,
        compiler_params=pltpu.CompilerParams(vmem_limit_bytes=LIMIT),
        **more,
    )


def groups(axes):
    made = {}
    for index in range(CHIPS_Z * SLAB):
        coordinate = {"z": index // SLAB, "y": index // CORES % CHIPS_Y, "c": index % CORES}
        made.setdefault(tuple(v for k, v in coordinate.items() if k not in axes), []).append(index)
    return list(made.values())


def swap_cores(array):
    pairs = [(index, index ^ 1) for index in range(CHIPS_Z * SLAB)]
    return lax.ppermute(array, "ctx", pairs)


def pass_on(array, step, way):
    pairs = []
    for index in range(CHIPS_Z * SLAB):
        there = index // SLAB + way
        source = (there - way * step) % CHIPS_Z
        needed = there >= step if way == 1 else source < CHIPS_Z // 2 - 1
        if needed and there < CHIPS_Z:
            pairs.append((index, there % CHIPS_Z * SLAB + index % SLAB))
    return lax.ppermute(array, "ctx", pairs)


LONG = pl.CostEstimate(flops=3 * 10**10, bytes_accessed=2**20, transcendentals=0)
COST = pl.CostEstimate(flops=3 * 10**9, bytes_accessed=2**20, transcendentals=2**20)


def local(head_count, query_rows, key_rows, value_rows, out_gain):
    index = lax.axis_index("ctx")
    place = jnp.stack([index >> 3, (index >> 1) & (CHIPS_Y - 1), index & 1]).astype(jnp.int32)

    summary_rows = [pl.BlockSpec((SUMMARY, 2 * HALF), lambda _, block=block: (block, 0)) for block in (15, 31)]
    packed = pl.pallas_call(
        pack_summary,
        grid=(1,),
        out_shape=jax.ShapeDtypeStruct((SLAB, 4 * SUMMARY, HALF), BF16),
        in_specs=summary_rows * 2,
        out_specs=pl.BlockSpec((SLAB, 4 * SUMMARY, HALF), lambda _: (0, 0, 0)),
    )(key_rows, key_rows, value_rows, value_rows)
    slab = lax.all_to_all(packed, "ctx", 0, 0, axis_index_groups=groups("yc"), tiled=True)
    query_rows, key_rows, value_rows, _ = lax.optimization_barrier((query_rows, key_rows, value_rows, packed))
    to_other = call(pack_other, jax.ShapeDtypeStruct((3 * ROWS, HALF), BF16), [SMEM] + [VMEM] * 3)(
        place, query_rows, key_rows, value_rows
    )
    from_other = swap_cores(to_other)
    gain = call(gain_columns, jax.ShapeDtypeStruct((2, HEAD_DIM, 8), F32), [SMEM, VMEM], cost=LONG)(place, out_gain[None])

    def attention(virtuals):
        return (
            jax.ShapeDtypeStruct((virtuals, ROWS, HEAD_DIM), BF16),
            jax.ShapeDtypeStruct((virtuals, 1, ROWS), F32),
            jax.ShapeDtypeStruct((virtuals, 1, ROWS), F32),
            jax.ShapeDtypeStruct((virtuals, HEAD_DIM, ROWS), F32),
        )

    state = attention(VIRTUAL)[1:]
    up, down, arrived = slab, slab, []
    for step in range(1, 5):
        if step == 1:
            up, down, gain = lax.optimization_barrier((up, down, gain))
        else:
            if step < 4:
                down, now = lax.optimization_barrier((down, now))
            else:
                up, now = lax.optimization_barrier((up, now))
        if step == 4:
            up = pass_on(up, step, 1)
        else:
            up, down = pass_on(up, step, 1), pass_on(down, step, -1)
        if step == 1:
            queries, *now = call(start_attention, attention(VIRTUAL), [SMEM] + [VMEM] * 5, cost=COST)(
                place, query_rows, key_rows, value_rows, from_other, slab
            )
        else:
            now = call(
                functools.partial(go_on, step - 1),
                state,
                [SMEM] + [VMEM] * 6,
                cost=COST,
                input_output_aliases={4 + i: i for i in range(3)},
            )(place, queries, *arrived[-1], *now)
        arrived.append((up, down))
    attended = jax.ShapeDtypeStruct((2, HEAD_DIM, ROWS), F32)
    own, other, squares = call(
        functools.partial(end_attention, 4),
        (attended, attended, jax.ShapeDtypeStruct((CORES, head_count, ROWS), F32)),
        [SMEM] + [VMEM] * 7,
        scratch=[pltpu.VMEM(part.shape, F32) for part in state],
    )(place, gain, queries, *arrived[3], *now)
    back = swap_cores(other)
    chips = [
        [(chip * CORES + core) * head_count + head for core in range(CORES) for head in range(head_count)]
        for chip in range(CHIPS_Z * CHIPS_Y)
    ]
    totals = lax.all_to_all(
        squares.reshape(CORES * head_count, ROWS), ("ctx", "head"), 0, 0, axis_index_groups=chips, tiled=True
    )
    return call(scale_rows, jax.ShapeDtypeStruct((ROWS, 4 * HEAD_DIM), BF16), [SMEM] + [VMEM] * 3)(
        place, own, back, totals
    )


def solution(mesh):
    placed = (P("ctx", "head"), P("ctx", "head"), P("ctx", "head"), P("head"))
    return jax.shard_map(
        functools.partial(local, mesh.shape["head"]),
        mesh=mesh,
        in_specs=placed,
        out_specs=P("ctx", "head"),
        check_vma=False,
    )
```

```python
import functools
import math

import jax
import jax.numpy as jnp
from jax import lax
from jax.experimental import pallas as pl
from jax.experimental.pallas import tpu as pltpu
from jax.sharding import PartitionSpec as P

HEAD_DIM = 128
BLOCK = 256
SUMMARY = 16
FEATURES = 4096
CHIPS_Z, CHIPS_Y, CORES = 8, 4, 2
SLAB = CHIPS_Y * CORES
HALF = 256
ROWS = 512
SCALE = HEAD_DIM**-0.5 * math.log2(math.e)
MINUS = -1e30
VIRTUAL = 4
VMEM = pl.BlockSpec(memory_space=pltpu.VMEM)
SMEM = pl.BlockSpec(memory_space=pltpu.SMEM)
LIMIT = 24 * 1024 * 1024

F32 = jnp.float32
BF16 = jnp.bfloat16


def rows_dot(a, b):
    return lax.dot_general(a, b, (((1,), (1,)), ((), ())), preferred_element_type=F32)


def columns_dot(a, b):
    return lax.dot_general(a, b, (((0,), (0,)), ((), ())), preferred_element_type=F32)


def pack_summary(*refs):
    *pieces, out_ref = refs
    for core in range(CORES):
        columns = slice(core * HALF, (core + 1) * HALF)
        for place, ref in enumerate(pieces):
            rows = slice(place * SUMMARY, (place + 1) * SUMMARY)
            for chip in range(CHIPS_Y):
                out_ref[chip * CORES + core, rows] = ref[:, columns]


def pack_other(place_ref, query_ref, key_ref, value_ref, out_ref):
    other = pl.multiple_of((1 - place_ref[2]) * HALF, HALF)
    for part, ref in enumerate((query_ref, key_ref, value_ref)):
        out_ref[part * ROWS : (part + 1) * ROWS] = ref[:, pl.ds(other, HALF)]


def slab_keys(slabs, head):
    columns = slice(head * HEAD_DIM, (head + 1) * HEAD_DIM)

    def joined(rows):
        return jnp.concatenate([slab[:, rows, columns].reshape(-1, HEAD_DIM) for slab in slabs])

    return joined(slice(0, 2 * SUMMARY)), joined(slice(2 * SUMMARY, 4 * SUMMARY))


def fold_slab(queries, state, slabs, first_blocks):
    max_ref, sum_ref, acc_ref = state
    parts = [slab_keys(slabs, head) for head in range(2)]
    staged = []
    for virtual in range(VIRTUAL):
        scores = rows_dot(parts[virtual % 2][0], queries[virtual]) * SCALE
        if first_blocks is not None:
            shape = scores.shape
            key_block = lax.broadcasted_iota(jnp.int32, shape, 0) // SUMMARY
            query_block = first_blocks[virtual // 2] + lax.broadcasted_iota(jnp.int32, shape, 1) // BLOCK
            scores = jnp.where(key_block < query_block, scores, MINUS)
        old_max = max_ref[virtual]
        new_max = jnp.maximum(old_max, jnp.max(scores, axis=0, keepdims=True))
        staged.append((jnp.exp2(scores - new_max), jnp.exp2(old_max - new_max)))
        max_ref[virtual] = new_max
    for virtual, (weights, shrink) in enumerate(staged):
        sum_ref[virtual] = sum_ref[virtual] * shrink + jnp.sum(weights, axis=0, keepdims=True)
        acc_ref[virtual] = acc_ref[virtual] * shrink + columns_dot(parts[virtual % 2][1], weights.astype(BF16))


def band(pieces, first, state, queries_ref):
    max_ref, sum_ref, acc_ref = state
    shape = (BLOCK, BLOCK)
    causal = lax.broadcasted_iota(jnp.int32, shape, 0) <= lax.broadcasted_iota(jnp.int32, shape, 1)
    staged = []
    for head in range(2):
        for block in range(2):
            virtual, rows = first + head, slice(block * BLOCK, (block + 1) * BLOCK)
            query, key, value = pieces(head, block)
            queries_ref[virtual, rows] = query
            scores = jnp.where(causal, rows_dot(key, query) * SCALE, MINUS)
            new_max = jnp.max(scores, axis=0, keepdims=True)
            max_ref[virtual, :, rows] = new_max
            staged.append((virtual, rows, value, jnp.exp2(scores - new_max)))
    for virtual, rows, value, weights in staged:
        sum_ref[virtual, :, rows] = jnp.sum(weights, axis=0, keepdims=True)
        acc_ref[virtual, :, rows] = columns_dot(value, weights.astype(BF16))


def gain_columns(place_ref, gain_ref, out_ref):
    mine = pl.multiple_of(place_ref[2] * HALF, HALF)
    for head in range(2):
        gain = gain_ref[:, pl.ds(mine + head * HEAD_DIM, HEAD_DIM)]
        out_ref[head] = jnp.transpose(jnp.broadcast_to(gain, (8, HEAD_DIM)))


def finish(core, gain_ref, state, own_ref, other_ref, square_ref):
    _, sum_ref, acc_ref = state
    for owner, ref in enumerate((own_ref, other_ref)):
        total = jnp.zeros((1, ROWS), F32)
        for head in range(2):
            virtual = owner * 2 + head
            attended = acc_ref[virtual] * (1.0 / sum_ref[virtual])
            ref[head] = attended * gain_ref[head, :, :1]
            total += jnp.sum(attended * attended, axis=0, keepdims=True)
        square_ref[core if owner == 0 else 1 - core] = jnp.broadcast_to(total, square_ref.shape[1:])


def start_attention(place_ref, query_ref, key_ref, value_ref, other_in_ref, slab_ref, queries_ref, *state):
    mine = pl.multiple_of(place_ref[2] * HALF, HALF)

    def own_pieces(head, block):
        rows, columns = slice(block * BLOCK, (block + 1) * BLOCK), pl.ds(mine + head * HEAD_DIM, HEAD_DIM)
        return (ref[rows, columns] for ref in (query_ref, key_ref, value_ref))

    def other_pieces(head, block):
        columns = slice(head * HEAD_DIM, (head + 1) * HEAD_DIM)
        starts = [part * ROWS + block * BLOCK for part in range(3)]
        return (other_in_ref[start : start + BLOCK, columns] for start in starts)

    band(own_pieces, 0, state, queries_ref)
    band(other_pieces, 2, state, queries_ref)
    chip, core = place_ref[1], place_ref[2]
    first_blocks = [(chip * CORES + core) * 2, (chip * CORES + 1 - core) * 2]
    fold_slab(queries_ref, state, [slab_ref], first_blocks)


def go_on(steps, place_ref, queries_ref, *refs):
    slabs, old_state, state = refs[: 2 * len(steps)], refs[2 * len(steps) : -3], refs[-3:]
    here = place_ref[0]
    for old_ref, ref in zip(old_state, state):
        ref[...] = old_ref[...]
    for turn, step in enumerate(steps):
        up_ref, down_ref = slabs[2 * turn : 2 * turn + 2]
        below, above = here >= step, here + step >= CHIPS_Z
        if step == 4:
            cases = ((below, [up_ref]),)
        elif step == 1:
            cases = ((below & ~above, [up_ref]), (below & above, [up_ref, down_ref]))
        else:
            cases = ((below & ~above, [up_ref]), (above & ~below, [down_ref]), (below & above, [up_ref, down_ref]))
        for reached, taken in cases:

            @pl.when(reached)
            def _(taken=taken):
                fold_slab(queries_ref, state, taken, None)


def end_attention(step, place_ref, gain_ref, queries_ref, up_ref, down_ref, *refs):
    old_state, outs, state = refs[:3], refs[3:6], refs[6:]
    go_on((step,), place_ref, queries_ref, up_ref, down_ref, *old_state, *state)
    finish(place_ref[2], gain_ref, state, *outs)


def scale_rows(place_ref, own_ref, other_ref, square_ref, out_ref):
    core = place_ref[2]
    total = jnp.sum(square_ref[...], axis=0, keepdims=True)
    scale = lax.rsqrt(total * (1.0 / FEATURES) + 1e-06)
    for owner, ref in enumerate((own_ref, other_ref)):
        first = pl.multiple_of((core if owner == 0 else 1 - core) * HALF, HALF)
        for head in range(2):
            columns = pl.ds(first + head * HEAD_DIM, HEAD_DIM)
            out_ref[:, columns] = jnp.transpose(ref[head] * scale).astype(BF16)


def call(body, out_shape, in_specs, scratch=(), cost=None, **more):
    outs = jax.tree.map(lambda _: VMEM, out_shape)
    return pl.pallas_call(
        body,
        out_shape=out_shape,
        in_specs=in_specs,
        out_specs=outs,
        scratch_shapes=list(scratch),
        cost_estimate=cost,
        compiler_params=pltpu.CompilerParams(vmem_limit_bytes=LIMIT),
        **more,
    )


def groups(axes):
    made = {}
    for index in range(CHIPS_Z * SLAB):
        coordinate = {"z": index // SLAB, "y": index // CORES % CHIPS_Y, "c": index % CORES}
        made.setdefault(tuple(v for k, v in coordinate.items() if k not in axes), []).append(index)
    return list(made.values())


def swap_cores(array):
    pairs = [(index, index ^ 1) for index in range(CHIPS_Z * SLAB)]
    return lax.ppermute(array, "ctx", pairs)


def pass_on(array, step, way):
    pairs = []
    for index in range(CHIPS_Z * SLAB):
        there = index // SLAB + way
        source = (there - way * step) % CHIPS_Z
        needed = there >= step if way == 1 else source < CHIPS_Z // 2 - 1
        if needed and there < CHIPS_Z:
            pairs.append((index, there % CHIPS_Z * SLAB + index % SLAB))
    return lax.ppermute(array, "ctx", pairs)


LONG = pl.CostEstimate(flops=3 * 10**10, bytes_accessed=2**20, transcendentals=0)
COST = pl.CostEstimate(flops=3 * 10**9, bytes_accessed=2**20, transcendentals=2**20)


def local(head_count, query_rows, key_rows, value_rows, out_gain):
    index = lax.axis_index("ctx")
    place = jnp.stack([index >> 3, (index >> 1) & (CHIPS_Y - 1), index & 1]).astype(jnp.int32)

    summary_rows = [pl.BlockSpec((SUMMARY, 2 * HALF), lambda _, block=block: (block, 0)) for block in (15, 31)]
    packed = pl.pallas_call(
        pack_summary,
        grid=(1,),
        out_shape=jax.ShapeDtypeStruct((SLAB, 4 * SUMMARY, HALF), BF16),
        in_specs=summary_rows * 2,
        out_specs=pl.BlockSpec((SLAB, 4 * SUMMARY, HALF), lambda _: (0, 0, 0)),
    )(key_rows, key_rows, value_rows, value_rows)
    slab = lax.all_to_all(packed, "ctx", 0, 0, axis_index_groups=groups("yc"), tiled=True)
    query_rows, key_rows, value_rows, _ = lax.optimization_barrier((query_rows, key_rows, value_rows, packed))
    to_other = call(pack_other, jax.ShapeDtypeStruct((3 * ROWS, HALF), BF16), [SMEM] + [VMEM] * 3)(
        place, query_rows, key_rows, value_rows
    )
    from_other = swap_cores(to_other)
    gain = call(gain_columns, jax.ShapeDtypeStruct((2, HEAD_DIM, 8), F32), [SMEM, VMEM], cost=LONG)(place, out_gain[None])

    def attention(virtuals):
        return (
            jax.ShapeDtypeStruct((virtuals, ROWS, HEAD_DIM), BF16),
            jax.ShapeDtypeStruct((virtuals, 1, ROWS), F32),
            jax.ShapeDtypeStruct((virtuals, 1, ROWS), F32),
            jax.ShapeDtypeStruct((virtuals, HEAD_DIM, ROWS), F32),
        )

    state = attention(VIRTUAL)[1:]
    up, down, arrived = slab, slab, []
    for step in range(1, 5):
        if step == 1:
            up, down, gain = lax.optimization_barrier((up, down, gain))
        else:
            if step == 2:
                down, now = lax.optimization_barrier((down, now))
            else:
                up, now = lax.optimization_barrier((up, now))
        if step == 4:
            up = pass_on(up, step, 1)
        else:
            up, down = pass_on(up, step, 1), pass_on(down, step, -1)
        if step == 1:
            queries, *now = call(start_attention, attention(VIRTUAL), [SMEM] + [VMEM] * 5, cost=COST)(
                place, query_rows, key_rows, value_rows, from_other, slab
            )
        elif step > 2:
            steps = (1,) if step == 3 else (2, 3)
            slabs = [part for past in steps for part in arrived[past - 1]]
            now = call(
                functools.partial(go_on, steps),
                state,
                [SMEM] + [VMEM] * (4 + len(slabs)),
                cost=COST,
                input_output_aliases={2 + len(slabs) + i: i for i in range(3)},
            )(place, queries, *slabs, *now)
        arrived.append((up, down))
    attended = jax.ShapeDtypeStruct((2, HEAD_DIM, ROWS), F32)
    own, other, squares = call(
        functools.partial(end_attention, 4),
        (attended, attended, jax.ShapeDtypeStruct((CORES, head_count, ROWS), F32)),
        [SMEM] + [VMEM] * 7,
        scratch=[pltpu.VMEM(part.shape, F32) for part in state],
    )(place, gain, queries, *arrived[3], *now)
    back = swap_cores(other)
    chips = [
        [(chip * CORES + core) * head_count + head for core in range(CORES) for head in range(head_count)]
        for chip in range(CHIPS_Z * CHIPS_Y)
    ]
    totals = lax.all_to_all(
        squares.reshape(CORES * head_count, ROWS), ("ctx", "head"), 0, 0, axis_index_groups=chips, tiled=True
    )
    return call(scale_rows, jax.ShapeDtypeStruct((ROWS, 4 * HEAD_DIM), BF16), [SMEM] + [VMEM] * 3)(
        place, own, back, totals
    )


def solution(mesh):
    placed = (P("ctx", "head"), P("ctx", "head"), P("ctx", "head"), P("head"))
    return jax.shard_map(
        functools.partial(local, mesh.shape["head"]),
        mesh=mesh,
        in_specs=placed,
        out_specs=P("ctx", "head"),
        check_vma=False,
    )
```

```python
import functools
import math

import jax
import jax.numpy as jnp
from jax import lax
from jax.experimental import pallas as pl
from jax.experimental.pallas import tpu as pltpu
from jax.sharding import PartitionSpec as P

HEAD_DIM = 128
BLOCK = 256
SUMMARY = 16
FEATURES = 4096
CHIPS_Z, CHIPS_Y, CORES = 8, 4, 2
SLAB = CHIPS_Y * CORES
HALF = 256
ROWS = 512
SCALE = HEAD_DIM**-0.5 * math.log2(math.e)
MINUS = -1e30
VIRTUAL = 4
VMEM = pl.BlockSpec(memory_space=pltpu.VMEM)
SMEM = pl.BlockSpec(memory_space=pltpu.SMEM)
LIMIT = 24 * 1024 * 1024

F32 = jnp.float32
BF16 = jnp.bfloat16


def rows_dot(a, b):
    return lax.dot_general(a, b, (((1,), (1,)), ((), ())), preferred_element_type=F32)


def columns_dot(a, b):
    return lax.dot_general(a, b, (((0,), (0,)), ((), ())), preferred_element_type=F32)


def pack_summary(*refs):
    *pieces, out_ref = refs
    for core in range(CORES):
        columns = slice(core * HALF, (core + 1) * HALF)
        for place, ref in enumerate(pieces):
            rows = slice(place * SUMMARY, (place + 1) * SUMMARY)
            for chip in range(CHIPS_Y):
                out_ref[chip * CORES + core, rows] = ref[:, columns]


def pack_other(place_ref, query_ref, key_ref, value_ref, out_ref):
    other = pl.multiple_of((1 - place_ref[2]) * HALF, HALF)
    for part, ref in enumerate((query_ref, key_ref, value_ref)):
        out_ref[part * ROWS : (part + 1) * ROWS] = ref[:, pl.ds(other, HALF)]


def slab_keys(slabs, head):
    columns = slice(head * HEAD_DIM, (head + 1) * HEAD_DIM)

    def joined(rows):
        return jnp.concatenate([slab[:, rows, columns].reshape(-1, HEAD_DIM) for slab in slabs])

    return joined(slice(0, 2 * SUMMARY)), joined(slice(2 * SUMMARY, 4 * SUMMARY))


def fold_slab(queries, state, slabs, first_blocks):
    max_ref, sum_ref, acc_ref = state
    parts = [slab_keys(slabs, head) for head in range(2)]
    staged = []
    for virtual in range(VIRTUAL):
        scores = rows_dot(parts[virtual % 2][0], queries[virtual]) * SCALE
        if first_blocks is not None:
            shape = scores.shape
            key_block = lax.broadcasted_iota(jnp.int32, shape, 0) // SUMMARY
            query_block = first_blocks[virtual // 2] + lax.broadcasted_iota(jnp.int32, shape, 1) // BLOCK
            scores = jnp.where(key_block < query_block, scores, MINUS)
        old_max = max_ref[virtual]
        new_max = jnp.maximum(old_max, jnp.max(scores, axis=0, keepdims=True))
        staged.append((jnp.exp2(scores - new_max), jnp.exp2(old_max - new_max)))
        max_ref[virtual] = new_max
    for virtual, (weights, shrink) in enumerate(staged):
        sum_ref[virtual] = sum_ref[virtual] * shrink + jnp.sum(weights, axis=0, keepdims=True)
        acc_ref[virtual] = acc_ref[virtual] * shrink + columns_dot(parts[virtual % 2][1], weights.astype(BF16))


def band(pieces, first, state, queries_ref):
    max_ref, sum_ref, acc_ref = state
    shape = (BLOCK, BLOCK)
    causal = lax.broadcasted_iota(jnp.int32, shape, 0) <= lax.broadcasted_iota(jnp.int32, shape, 1)
    staged = []
    for head in range(2):
        for block in range(2):
            virtual, rows = first + head, slice(block * BLOCK, (block + 1) * BLOCK)
            query, key, value = pieces(head, block)
            queries_ref[virtual, rows] = query
            scores = jnp.where(causal, rows_dot(key, query) * SCALE, MINUS)
            new_max = jnp.max(scores, axis=0, keepdims=True)
            max_ref[virtual, :, rows] = new_max
            staged.append((virtual, rows, value, jnp.exp2(scores - new_max)))
    for virtual, rows, value, weights in staged:
        sum_ref[virtual, :, rows] = jnp.sum(weights, axis=0, keepdims=True)
        acc_ref[virtual, :, rows] = columns_dot(value, weights.astype(BF16))


def gain_columns(place_ref, gain_ref, out_ref):
    mine = pl.multiple_of(place_ref[2] * HALF, HALF)
    for head in range(2):
        gain = gain_ref[:, pl.ds(mine + head * HEAD_DIM, HEAD_DIM)]
        out_ref[head] = jnp.transpose(jnp.broadcast_to(gain, (8, HEAD_DIM)))


def finish(core, gain_ref, state, own_ref, other_ref, square_ref):
    _, sum_ref, acc_ref = state
    for owner, ref in enumerate((own_ref, other_ref)):
        total = jnp.zeros((1, ROWS), F32)
        for head in range(2):
            virtual = owner * 2 + head
            attended = acc_ref[virtual] * (1.0 / sum_ref[virtual])
            ref[head] = attended * gain_ref[head, :, :1]
            total += jnp.sum(attended * attended, axis=0, keepdims=True)
        heads = square_ref.shape[0] // CORES
        first = (core if owner == 0 else 1 - core) * heads
        square_ref[pl.ds(first, heads)] = jnp.broadcast_to(total[None], (heads, 1, ROWS))


def start_attention(place_ref, query_ref, key_ref, value_ref, other_in_ref, slab_ref, queries_ref, *state):
    mine = pl.multiple_of(place_ref[2] * HALF, HALF)

    def own_pieces(head, block):
        rows, columns = slice(block * BLOCK, (block + 1) * BLOCK), pl.ds(mine + head * HEAD_DIM, HEAD_DIM)
        return (ref[rows, columns] for ref in (query_ref, key_ref, value_ref))

    def other_pieces(head, block):
        columns = slice(head * HEAD_DIM, (head + 1) * HEAD_DIM)
        starts = [part * ROWS + block * BLOCK for part in range(3)]
        return (other_in_ref[start : start + BLOCK, columns] for start in starts)

    band(own_pieces, 0, state, queries_ref)
    band(other_pieces, 2, state, queries_ref)
    chip, core = place_ref[1], place_ref[2]
    first_blocks = [(chip * CORES + core) * 2, (chip * CORES + 1 - core) * 2]
    fold_slab(queries_ref, state, [slab_ref], first_blocks)


def go_on(steps, place_ref, queries_ref, *refs):
    slabs, old_state, state = refs[: 2 * len(steps)], refs[2 * len(steps) : -3], refs[-3:]
    here = place_ref[0]
    for old_ref, ref in zip(old_state, state):
        ref[...] = old_ref[...]
    for turn, step in enumerate(steps):
        up_ref, down_ref = slabs[2 * turn : 2 * turn + 2]
        below, above = here >= step, here + step >= CHIPS_Z
        if step == 4:
            cases = ((below, [up_ref]),)
        elif step == 1:
            cases = ((below & ~above, [up_ref]), (below & above, [up_ref, down_ref]))
        else:
            cases = ((below & ~above, [up_ref]), (above & ~below, [down_ref]), (below & above, [up_ref, down_ref]))
        for reached, taken in cases:

            @pl.when(reached)
            def _(taken=taken):
                fold_slab(queries_ref, state, taken, None)


def end_attention(step, place_ref, gain_ref, queries_ref, up_ref, down_ref, *refs):
    old_state, outs, state = refs[:3], refs[3:6], refs[6:]
    go_on((step,), place_ref, queries_ref, up_ref, down_ref, *old_state, *state)
    finish(place_ref[2], gain_ref, state, *outs)


def scale_rows(place_ref, own_ref, other_ref, square_ref, out_ref):
    core = place_ref[2]
    total = jnp.sum(square_ref[...], axis=0)
    scale = lax.rsqrt(total * (1.0 / FEATURES) + 1e-06)
    for owner, ref in enumerate((own_ref, other_ref)):
        first = pl.multiple_of((core if owner == 0 else 1 - core) * HALF, HALF)
        for head in range(2):
            columns = pl.ds(first + head * HEAD_DIM, HEAD_DIM)
            out_ref[:, columns] = jnp.transpose(ref[head] * scale).astype(BF16)


def call(body, out_shape, in_specs, scratch=(), cost=None, **more):
    outs = jax.tree.map(lambda _: VMEM, out_shape)
    return pl.pallas_call(
        body,
        out_shape=out_shape,
        in_specs=in_specs,
        out_specs=outs,
        scratch_shapes=list(scratch),
        cost_estimate=cost,
        compiler_params=pltpu.CompilerParams(vmem_limit_bytes=LIMIT),
        **more,
    )


def groups(axes):
    made = {}
    for index in range(CHIPS_Z * SLAB):
        coordinate = {"z": index // SLAB, "y": index // CORES % CHIPS_Y, "c": index % CORES}
        made.setdefault(tuple(v for k, v in coordinate.items() if k not in axes), []).append(index)
    return list(made.values())


def swap_cores(array):
    pairs = [(index, index ^ 1) for index in range(CHIPS_Z * SLAB)]
    return lax.ppermute(array, "ctx", pairs)


def pass_on(array, step, way):
    pairs = []
    for index in range(CHIPS_Z * SLAB):
        there = index // SLAB + way
        source = (there - way * step) % CHIPS_Z
        needed = there >= step if way == 1 else source < CHIPS_Z // 2 - 1
        if needed and there < CHIPS_Z:
            pairs.append((index, there % CHIPS_Z * SLAB + index % SLAB))
    return lax.ppermute(array, "ctx", pairs)


LONG = pl.CostEstimate(flops=3 * 10**10, bytes_accessed=2**20, transcendentals=0)
COST = pl.CostEstimate(flops=3 * 10**9, bytes_accessed=2**20, transcendentals=2**20)


def local(head_count, query_rows, key_rows, value_rows, out_gain):
    index = lax.axis_index("ctx")
    place = jnp.stack([index >> 3, (index >> 1) & (CHIPS_Y - 1), index & 1]).astype(jnp.int32)

    summary_rows = [pl.BlockSpec((SUMMARY, 2 * HALF), lambda _, block=block: (block, 0)) for block in (15, 31)]
    packed = pl.pallas_call(
        pack_summary,
        grid=(1,),
        out_shape=jax.ShapeDtypeStruct((SLAB, 4 * SUMMARY, HALF), BF16),
        in_specs=summary_rows * 2,
        out_specs=pl.BlockSpec((SLAB, 4 * SUMMARY, HALF), lambda _: (0, 0, 0)),
    )(key_rows, key_rows, value_rows, value_rows)
    slab = lax.all_to_all(packed, "ctx", 0, 0, axis_index_groups=groups("yc"), tiled=True)
    query_rows, key_rows, value_rows, _ = lax.optimization_barrier((query_rows, key_rows, value_rows, packed))
    to_other = call(pack_other, jax.ShapeDtypeStruct((3 * ROWS, HALF), BF16), [SMEM] + [VMEM] * 3)(
        place, query_rows, key_rows, value_rows
    )
    from_other = swap_cores(to_other)
    gain = call(gain_columns, jax.ShapeDtypeStruct((2, HEAD_DIM, 8), F32), [SMEM, VMEM], cost=LONG)(place, out_gain[None])

    def attention(virtuals):
        return (
            jax.ShapeDtypeStruct((virtuals, ROWS, HEAD_DIM), BF16),
            jax.ShapeDtypeStruct((virtuals, 1, ROWS), F32),
            jax.ShapeDtypeStruct((virtuals, 1, ROWS), F32),
            jax.ShapeDtypeStruct((virtuals, HEAD_DIM, ROWS), F32),
        )

    state = attention(VIRTUAL)[1:]
    up, down, arrived = slab, slab, []
    for step in range(1, 5):
        if step == 1:
            up, down, gain = lax.optimization_barrier((up, down, gain))
        else:
            if step == 2:
                down, now = lax.optimization_barrier((down, now))
            else:
                up, now = lax.optimization_barrier((up, now))
        if step == 4:
            up = pass_on(up, step, 1)
        else:
            up, down = pass_on(up, step, 1), pass_on(down, step, -1)
        if step == 1:
            queries, *now = call(start_attention, attention(VIRTUAL), [SMEM] + [VMEM] * 5, cost=COST)(
                place, query_rows, key_rows, value_rows, from_other, slab
            )
        elif step > 2:
            steps = (1,) if step == 3 else (2, 3)
            slabs = [part for past in steps for part in arrived[past - 1]]
            now = call(
                functools.partial(go_on, steps),
                state,
                [SMEM] + [VMEM] * (4 + len(slabs)),
                cost=COST,
                input_output_aliases={2 + len(slabs) + i: i for i in range(3)},
            )(place, queries, *slabs, *now)
        arrived.append((up, down))
    attended = jax.ShapeDtypeStruct((2, HEAD_DIM, ROWS), F32)
    own, other, squares = call(
        functools.partial(end_attention, 4),
        (attended, attended, jax.ShapeDtypeStruct((CORES * head_count, 1, ROWS), F32)),
        [SMEM] + [VMEM] * 7,
        scratch=[pltpu.VMEM(part.shape, F32) for part in state],
    )(place, gain, queries, *arrived[3], *now)
    back = swap_cores(other)
    chips = [
        [(chip * CORES + core) * head_count + head for core in range(CORES) for head in range(head_count)]
        for chip in range(CHIPS_Z * CHIPS_Y)
    ]
    totals = lax.all_to_all(
        squares, ("ctx", "head"), 0, 0, axis_index_groups=chips, tiled=True
    )
    return call(scale_rows, jax.ShapeDtypeStruct((ROWS, 4 * HEAD_DIM), BF16), [SMEM] + [VMEM] * 3)(
        place, own, back, totals
    )


def solution(mesh):
    placed = (P("ctx", "head"), P("ctx", "head"), P("ctx", "head"), P("head"))
    return jax.shard_map(
        functools.partial(local, mesh.shape["head"]),
        mesh=mesh,
        in_specs=placed,
        out_specs=P("ctx", "head"),
        check_vma=False,
    )
```
